512 devices in a mesh: dp: 16 (over y, core), group: 32 (over x, z).
Axes of the slice: x: 4, y: 8, z: 8, core: 2. Of those that a mesh axis runs over, the one named last changes fastest.
Arguments:
- partial_stats: bfloat16 [16, 16, 1024, 1024], P('dp', None, 'group'), as said below
- old_basis: bfloat16 [16, 2, 1024, 1024], P('dp', None, 'group'), as said below
- exp_avg: float32 [16, 2, 1024, 4096], P('dp', None, None, 'group'), may hold values from -6 to 6
- slot_block: int32 [16, 2], replicated, may hold values from -1 to 15, as said below
Outputs:
- exp_avg_new: float32 [16, 2, 1024, 4096], P('dp', None, None, 'group')
The draws below stay inside these ranges and needn't reach their ends.
Inputs may be any that keep to these rules, and one draw needn't show every extreme that they name: `slot_block`: row d lists the blocks refreshed by data-parallel row d, used slots first and -1 in the rest; every block 0 to 15 stands in exactly one slot. Some row uses all 2 slots and some row none. `partial_stats`: each replica's share is symmetric; the sum over replicas of one block is symmetric positive definite. `old_basis`: each matrix is well conditioned.
All inputs are finite; a program needn't handle non-finite values.
Results may differ from the reference program's by a relative error of at most 0.015.
Values may be sent and summed in bfloat16 or wider, within the bound.
No kernel may reach another device: no remote copies, remote signals or barrier semaphores. Data moves between devices by JAX's collectives and lax.ppermute only.
A program may use at most 64 MiB of HBM per device.

```python
import math
import jax
import jax.numpy as jnp
from jax import lax

BLK = 1024
WCOLS = 4096
BPR = 1
CAP = 2
NB = 16
N_DP = 16


def draw_partial_stats(key, part):
    key = jax.random.fold_in(key, 11)
    first_key, second_key = jax.random.split(key, 2)
    replica_scale = 1.0 + 2.0 * jnp.arange(N_DP, dtype=jnp.float32) / (N_DP - 1)
    scale_sum = 2.0 * N_DP
    square_sum = sum(((1.0 + 2.0 * index_value / (N_DP - 1)) ** 2 for index_value in range(N_DP)))
    spread_value = 0.6 * scale_sum / (math.sqrt(square_sum) * math.sqrt(BLK))
    diagonal = jax.random.uniform(first_key, (N_DP, NB, BLK), jnp.float32, 2.0, 4.0)
    raw_noise = jax.random.normal(second_key, (N_DP, NB, BLK, BLK), jnp.float32)
    symmetric_noise = (raw_noise + jnp.swapaxes(raw_noise, 2, 3)) * (spread_value / math.sqrt(2.0))
    diagonal_mask = (jnp.arange(BLK)[:, None] == jnp.arange(BLK)[None, :]).astype(jnp.float32)
    matrix = symmetric_noise + diagonal[..., None] * diagonal_mask
    return (replica_scale[:, None, None, None] * matrix / N_DP).astype(jnp.bfloat16)


def draw_old_basis(key, part):
    key = jax.random.fold_in(key, 17)
    spread_value = 0.3 / math.sqrt(BLK)
    raw_noise = jax.random.normal(key, (N_DP, CAP, BLK, BLK), jnp.float32)
    diagonal_mask = (jnp.arange(BLK)[:, None] == jnp.arange(BLK)[None, :]).astype(jnp.float32)
    return (diagonal_mask + spread_value * raw_noise).astype(jnp.bfloat16)


def draw_slot_block(key, part):
    key = jax.random.fold_in(key, 29)
    first_key, second_key, third_key = jax.random.split(key, 3)
    row_order = jax.random.permutation(first_key, N_DP)
    row_rank = jnp.argsort(row_order)
    full_rows = jax.random.randint(second_key, (), 1, N_DP // 2 + 1)
    row_counts = jnp.where(row_rank < full_rows, CAP, jnp.where(row_rank < 2 * full_rows, 0, BPR))
    row_starts = jnp.cumsum(row_counts) - row_counts
    block_order = jax.random.permutation(third_key, NB)
    slot_position = jnp.arange(CAP)
    list_index = jnp.clip(row_starts[:, None] + slot_position[None, :], 0, NB - 1)
    is_filled = slot_position[None, :] < row_counts[:, None]
    return jnp.where(is_filled, block_order[list_index], -1).astype(jnp.int32)


def steps_of(rng, extent, pieces, low, largest):
    loudness = 1.0
    for axis_at, shards_of in pieces:
        heights = jax.random.uniform(jax.random.fold_in(jax.random.fold_in(rng, 6), axis_at), (shards_of,), jnp.float32, low / len(pieces), largest / len(pieces))
        loudness = loudness * jnp.repeat(jnp.exp(heights), extent[axis_at] // shards_of).reshape((-1,) + (1,) * (len(extent) - 1 - axis_at))
    return loudness


def noise(stream_key, shape, deviation, most, shards=(), kind=jnp.bfloat16):
    level = steps_of(stream_key, shape, shards, -0.22, 0.18) if shards else 1.0
    drawn = jax.random.normal(stream_key, shape, jnp.float32) * deviation * level
    return jnp.minimum(jnp.maximum(drawn, -most), most).astype(kind)


def setup_inputs(seed: int = 0) -> dict:
    seeds = jax.random.split(jax.random.key(seed), 5)
    return {
        "partial_stats": draw_partial_stats(jax.random.fold_in(seeds[4], 71), 0),
        "old_basis": draw_old_basis(jax.random.fold_in(seeds[4], 71), 0),
        "exp_avg": noise(seeds[2], (N_DP, CAP, BLK, WCOLS), 1.0, 6.0, ((0, 16), (3, 32)), jnp.float32),
        "slot_block": draw_slot_block(jax.random.fold_in(seeds[4], 71), 0),
    }


def reference(partial_stats, old_basis, exp_avg, slot_block):
    flat_blocks = slot_block.reshape(-1)
    old_flat = old_basis.reshape(N_DP * CAP, BLK, BLK)
    moment_flat = exp_avg.reshape(N_DP * CAP, BLK, WCOLS)
    identity = jnp.eye(BLK, dtype=jnp.float32)

    def refresh_one(operands):
        block_id, previous_raw, moment = operands
        slot_live = block_id >= 0
        block_index = jnp.maximum(block_id, 0).astype(jnp.int32)
        chosen = lax.dynamic_index_in_dim(partial_stats, block_index, 1, keepdims=False)
        factor = jnp.sum(chosen.astype(jnp.float32), axis=0)
        factor = jnp.where(slot_live, factor, identity)
        factor_low = factor.astype(jnp.bfloat16)
        previous = jnp.where(slot_live, previous_raw, identity.astype(jnp.bfloat16))
        projected = jnp.dot(factor_low.astype(jnp.float32), previous.astype(jnp.float32), preferred_element_type=jnp.float32).astype(jnp.bfloat16)
        gram_total = jnp.dot(projected.T.astype(jnp.float32), projected.astype(jnp.float32), preferred_element_type=jnp.float32)
        lower_factor = jnp.linalg.cholesky(gram_total)
        solved = jax.scipy.linalg.solve_triangular(lower_factor, projected.astype(jnp.float32).T, lower=True)
        new_basis = solved.T.astype(jnp.bfloat16)
        back_moment = jnp.dot(previous.astype(jnp.float32), moment, precision=lax.Precision.HIGHEST)
        rotated = jnp.dot(new_basis.astype(jnp.float32).T, back_moment, precision=lax.Precision.HIGHEST)
        return jnp.where(slot_live, rotated, jnp.zeros_like(rotated))
    rotated_all = lax.map(refresh_one, (flat_blocks, old_flat, moment_flat))
    return rotated_all.reshape(N_DP, CAP, BLK, WCOLS)
```

```python
import functools

import jax
import jax.numpy as jnp
from jax import lax
from jax.experimental import pallas as pl
from jax.experimental.pallas import tpu as pltpu
from jax.sharding import PartitionSpec as P

BF16, F32 = jnp.bfloat16, jnp.float32
VMEM_BYTES = 48 * 1024 * 1024
TILE = 128
SUB = 8
X_CHIPS, Z_CHIPS = 4, 8


def high_low(value):
    high = value.astype(BF16)
    return high, (value - high.astype(F32)).astype(BF16)


def from_neighbour(value, dx, dz):
    pairs = []
    for x in range(X_CHIPS):
        for z in range(Z_CHIPS):
            source = (x + dx) % X_CHIPS * Z_CHIPS + (z + dz) % Z_CHIPS
            pairs.append((source, x * Z_CHIPS + z))
    return lax.ppermute(value, "group", pairs)


def gather_rows(slab):
    pieces = [slab] + [None] * (Z_CHIPS - 1)
    for dz in (1, -1, 2, -2):
        pieces[dz % Z_CHIPS] = from_neighbour(slab, 0, dz)
    pieces[3] = from_neighbour(pieces[2], 0, 1)
    pieces[5] = from_neighbour(pieces[6], 0, -1)
    far_first = from_neighbour(pieces[2][:1], 0, 2)
    far_second = from_neighbour(pieces[6][1:], 0, -2)
    pieces[4] = jnp.concatenate([far_first, far_second], axis=0)
    own = jnp.stack(pieces, axis=1).reshape(2, Z_CHIPS * slab.shape[1], slab.shape[2])
    after = from_neighbour(own, 1, 0)
    before = from_neighbour(own, -1, 0)
    across_first = from_neighbour(after[0], 1, 0)
    across_second = from_neighbour(before[1], -1, 0)
    return own, after, across_first, across_second, before


def quarter(refs, slot, distance):
    own, after, across_first, across_second, before = refs
    if distance == 2:
        return (across_first, across_second)[slot][...]
    return (own, after, None, before)[distance][slot]


def back_kernel(*refs):
    rows, moment, out = refs[:5], refs[5], refs[6]
    for slot in range(2):
        high, low = high_low(moment[slot])
        both = jnp.concatenate([high, low], axis=1)
        for distance in range(X_CHIPS):
            block = quarter(rows, slot, distance)
            size = block.shape[0]
            product = jnp.dot(block, both, preferred_element_type=F32)
            width = high.shape[1]
            high_back, low_back = high_low(product[:, :width] + product[:, width:])
            out[slot, distance * size : (distance + 1) * size, :] = jnp.concatenate([high_back, low_back], axis=1)


def project_kernel(place, factor, *refs):
    rows, out = refs[:5], refs[5]
    x, z = place[0], place[1]
    for slot in range(2):
        total = jnp.zeros(out.shape[1:], F32)
        for distance in range(X_CHIPS):
            block = quarter(rows, slot, distance)
            size = block.shape[0]
            at = lax.rem(x + distance, X_CHIPS) * size
            part = factor[slot, :, pl.ds(pl.multiple_of(at, size), size)].astype(F32)
            step = size // Z_CHIPS
            part = pltpu.roll(part, lax.rem((Z_CHIPS - z) * step, size), 1)
            total += jnp.dot(part.astype(BF16), block, preferred_element_type=F32)
        out[slot] = total.astype(BF16)


def row_of(value, at):
    return jnp.broadcast_to(value[at : at + 1, :], value.shape)


def lane_of(value, at):
    return jnp.broadcast_to(value[:, at : at + 1], value.shape)


def inverse_factors(work, inverse):
    lane = lax.broadcasted_iota(jnp.int32, (SUB, TILE), 1)
    upper_half = lax.broadcasted_iota(jnp.int32, (SUB, TILE), 0) < SUB // 2
    n_sub = TILE // SUB
    tiles = [[work[slot, SUB * i : SUB * (i + 1), :] for i in range(n_sub)] for slot in range(2)]
    for s in range(n_sub):
        first = SUB * s
        inside = (lane >= first) & (lane < first + SUB)
        rows = [jnp.where(upper_half, row_of(tiles[0][s], r), row_of(tiles[1][s], r)) for r in range(SUB)]
        entry = [[lane_of(rows[r], first + c) for c in range(r + 1)] for r in range(SUB)]
        rows = [jnp.where(inside, jnp.where(lane == first + r, 1.0, 0.0), rows[r]) for r in range(SUB)]
        ratio = [[None] * SUB for _ in range(SUB)]
        inverse_pivot = [None] * SUB
        for k in range(SUB):
            inverse_pivot[k] = 1.0 / entry[k][k]
            for r in range(k + 1, SUB):
                ratio[r][k] = entry[r][k] * inverse_pivot[k]
            for r in range(k + 1, SUB):
                for c in range(k + 1, r + 1):
                    entry[r][c] = entry[r][c] - ratio[r][k] * entry[c][k]
                rows[r] = rows[r] - ratio[r][k] * rows[k]
        solved = [None] * SUB
        for k in reversed(range(SUB)):
            value = rows[k] * inverse_pivot[k]
            for r in reversed(range(k + 1, SUB)):
                value = value - ratio[r][k] * solved[r]
            solved[k] = value
        for k in range(SUB):
            scaled = jnp.where(lane < first + SUB, rows[k] * lax.rsqrt(entry[k][k]), 0.0)
            for slot in range(2):
                at = slot * (SUB // 2)
                inverse[slot, first + k : first + k + 1, :] = scaled[at : at + 1, :]
        if s + 1 == n_sub:
            break
        for slot in range(2):
            spread = [row_of(solved[k], slot * (SUB // 2)) for k in range(SUB)]
            for i in range(s + 1, n_sub):
                old = tiles[slot][i]
                terms = [lane_of(old, first + c) * spread[c] for c in range(SUB)]
                while len(terms) > 1:
                    terms = [a + b for a, b in zip(terms[::2], terms[1::2])]
                tiles[slot][i] = jnp.where(inside, 0.0, old) - terms[0]


def eliminate_kernel(live, *refs):
    rows, back, out = refs[:5], refs[5], refs[6]
    projected, system, work, inverse, panel, panel_high_low = refs[7:]
    order = projected.shape[1]
    blocks = order // TILE
    width = out.shape[2]
    for slot in range(2):
        for distance in range(X_CHIPS):
            block = quarter(rows, slot, distance)
            size = block.shape[0]
            projected[slot, distance * size : (distance + 1) * size, :] = block

    def normal_equations(j, carry):
        for slot in range(2):
            columns = projected[slot, :, pl.ds(pl.multiple_of(j * TILE, TILE), TILE)].T
            system[slot, j, :, :order] = jnp.dot(columns, projected[slot], preferred_element_type=F32)
            right = jnp.dot(columns, back[slot], preferred_element_type=F32)
            system[slot, j, :, order:] = right[:, :width] + right[:, width:]
        return carry

    lax.fori_loop(0, blocks, normal_equations, 0)

    def step(j, carry):
        here = pl.ds(pl.multiple_of(j * TILE, TILE), TILE)
        for slot in range(2):
            work[slot] = system[slot, j, :, here]
        inverse_factors(work, inverse)
        for slot in range(2):
            high, low = high_low(inverse[slot])
            left = jnp.concatenate([high, high, low], axis=1)
            high, low = high_low(system[slot, j])
            right = jnp.concatenate([high, low, high], axis=0)
            solved = jnp.dot(left, right, preferred_element_type=F32)
            panel[slot] = solved
            high, low = high_low(solved)
            panel_high_low[slot] = jnp.concatenate([high, low, high], axis=0)
            out[slot, here, :] = jnp.where(live[slot] >= 0, solved[:, order:], 0.0)

        def trail(i, inner):
            for slot in range(2):
                columns = panel[slot, :, pl.ds(pl.multiple_of(i * TILE, TILE), TILE)].T
                high, low = high_low(columns)
                left = jnp.concatenate([high, high, low], axis=1)
                system[slot, i] -= jnp.dot(left, panel_high_low[slot], preferred_element_type=F32)
            return inner

        lax.fori_loop(j + 1, blocks, trail, 0)
        return carry

    lax.fori_loop(0, blocks, step, 0)


def back_moments(rows, moment):
    order, width = moment.shape[1:]
    return pl.pallas_call(
        back_kernel,
        out_shape=jax.ShapeDtypeStruct((2, order, 2 * width), BF16),
        compiler_params=pltpu.CompilerParams(vmem_limit_bytes=VMEM_BYTES),
        cost_estimate=pl.CostEstimate(flops=8 * order * order * width, bytes_accessed=6 << 20, transcendentals=0),
        name="back_moments",
    )(*rows, moment)


def project(place, factor, rows):
    smem = pl.BlockSpec(memory_space=pltpu.SMEM)
    vmem = pl.BlockSpec(memory_space=pltpu.VMEM)
    return pl.pallas_call(
        project_kernel,
        out_shape=jax.ShapeDtypeStruct(factor.shape, BF16),
        in_specs=[smem] + [vmem] * 6,
        out_specs=vmem,
        compiler_params=pltpu.CompilerParams(vmem_limit_bytes=VMEM_BYTES),
        cost_estimate=pl.CostEstimate(flops=2 * factor.size * factor.shape[2], bytes_accessed=5 << 20, transcendentals=0),
        name="project",
    )(place, factor, *rows)


def eliminate(live, rows, back):
    _, order, twice = back.shape
    width = twice // 2
    smem = pl.BlockSpec(memory_space=pltpu.SMEM)
    vmem = pl.BlockSpec(memory_space=pltpu.VMEM)
    return pl.pallas_call(
        eliminate_kernel,
        out_shape=jax.ShapeDtypeStruct((2, order, width), F32),
        in_specs=[smem] + [vmem] * 6,
        out_specs=vmem,
        scratch_shapes=[
            pltpu.VMEM((2, order, order), BF16),
            pltpu.VMEM((2, order // TILE, TILE, order + width), F32),
            pltpu.VMEM((2, TILE, TILE), F32),
            pltpu.VMEM((2, TILE, TILE), F32),
            pltpu.VMEM((2, TILE, order + width), F32),
            pltpu.VMEM((2, 3 * TILE, order + width), BF16),
        ],
        compiler_params=pltpu.CompilerParams(vmem_limit_bytes=VMEM_BYTES),
        cost_estimate=pl.CostEstimate(flops=6 * order**3, bytes_accessed=6 << 20, transcendentals=0),
        name="eliminate",
    )(live, *rows, back)


def on_device(partial_stats, old_basis, exp_avg, slot_block):
    slab_rows, order = partial_stats.shape[2:]
    n_rows = slot_block.shape[0]
    group = lax.axis_index("group")
    own_slots = lax.dynamic_index_in_dim(slot_block, lax.axis_index("dp"), 0, keepdims=False)
    live = (own_slots >= 0)[:, None, None]
    row = lax.broadcasted_iota(jnp.int32, (slab_rows, order), 0) + group * slab_rows
    column = lax.broadcasted_iota(jnp.int32, (slab_rows, order), 1)
    identity = (row == column).astype(F32)[None]

    previous = jnp.where(live, old_basis[0], identity.astype(BF16))
    previous_rows = gather_rows(previous)

    sent = jnp.take(partial_stats[0], jnp.maximum(slot_block.reshape(-1), 0), axis=0)
    sent = sent.reshape(n_rows, 2, slab_rows, order)
    shares = lax.all_to_all(sent, "dp", split_axis=0, concat_axis=0)
    factor = jnp.where(live, jnp.sum(shares.astype(F32), axis=0), identity).astype(BF16)

    place = jnp.stack([group // Z_CHIPS, group % Z_CHIPS]).astype(jnp.int32)
    projected_rows = gather_rows(project(place, factor, previous_rows))
    back = back_moments(previous_rows, exp_avg[0])
    return eliminate(own_slots, projected_rows, back)[None]


def solution(mesh):
    return jax.shard_map(
        on_device,
        mesh=mesh,
        in_specs=(
            P("dp", None, "group", None),
            P("dp", None, "group", None),
            P("dp", None, None, "group"),
            P(),
        ),
        out_specs=P("dp", None, None, "group"),
        check_vma=False,
    )
```

```python
import functools

import jax
import jax.numpy as jnp
from jax import lax
from jax.experimental import pallas as pl
from jax.experimental.pallas import tpu as pltpu
from jax.sharding import PartitionSpec as P

BF16, F32 = jnp.bfloat16, jnp.float32
VMEM_BYTES = 48 * 1024 * 1024
TILE = 128
SUB = 8
X_CHIPS, Z_CHIPS = 4, 8


def high_low(value):
    high = value.astype(BF16)
    return high, (value - high.astype(F32)).astype(BF16)


def from_neighbour(value, dx, dz):
    pairs = []
    for x in range(X_CHIPS):
        for z in range(Z_CHIPS):
            source = (x + dx) % X_CHIPS * Z_CHIPS + (z + dz) % Z_CHIPS
            pairs.append((source, x * Z_CHIPS + z))
    return lax.ppermute(value, "group", pairs)


def gather_factor(slab):
    rows_of_z = [[x * Z_CHIPS + z for z in range(Z_CHIPS)] for x in range(X_CHIPS)]
    copies = jnp.broadcast_to(slab[None], (Z_CHIPS,) + slab.shape)
    own = lax.all_to_all(copies, "group", split_axis=0, concat_axis=0, axis_index_groups=rows_of_z)
    after = from_neighbour(own, 1, 0)
    before = from_neighbour(own, -1, 0)
    half = Z_CHIPS // 2
    across_low = from_neighbour(after[:half], 1, 0)
    across_high = from_neighbour(before[half:], -1, 0)
    return own, after, across_low, across_high, before


def back_kernel(basis, moment, out):
    width = moment.shape[2]
    order = out.shape[1]
    for slot in range(2):
        high, low = high_low(moment[slot])
        both = jnp.concatenate([high, low], axis=1)
        product = jnp.dot(basis[:, slot].reshape(order, order), both, preferred_element_type=F32)
        high, low = high_low(product[:, :width] + product[:, width:])
        out[slot] = jnp.concatenate([high, low], axis=1)


def fill_factor(x, pieces, factor):
    own, after, across_low, across_high, before = pieces
    half = Z_CHIPS // 2
    blocks = factor.shape[1] // TILE
    for distance in range(X_CHIPS):
        for z_half in range(2):
            block_row = lax.rem(x + distance, X_CHIPS) * 2 + z_half
            here = pl.ds(pl.multiple_of(block_row * TILE, TILE), TILE)
            for slot in range(2):
                if distance == 2:
                    piece = (across_low, across_high)[z_half][:, slot]
                else:
                    piece = (own, after, None, before)[distance][half * z_half : half * (z_half + 1), slot]
                piece = piece.reshape(TILE, piece.shape[2])
                for k in range(blocks // 2 + 1):
                    there = pl.ds(pl.multiple_of(lax.rem(block_row + k, blocks) * TILE, TILE), TILE)
                    block = piece[:, TILE * k : TILE * (k + 1)]
                    factor[slot, here, there] = block
                    if 0 < k < blocks // 2:
                        factor[slot, there, here] = block.T


def row_of(value, at):
    return jnp.broadcast_to(value[at : at + 1, :], value.shape)


def lane_of(value, at):
    return jnp.broadcast_to(value[:, at : at + 1], value.shape)


def inverse_factors(work, inverse):
    lane = lax.broadcasted_iota(jnp.int32, (SUB, TILE), 1)
    upper_half = lax.broadcasted_iota(jnp.int32, (SUB, TILE), 0) < SUB // 2
    n_sub = TILE // SUB
    tiles = [[work[slot, SUB * i : SUB * (i + 1), :] for i in range(n_sub)] for slot in range(2)]
    for s in range(n_sub):
        first = SUB * s
        inside = (lane >= first) & (lane < first + SUB)
        rows = [jnp.where(upper_half, row_of(tiles[0][s], r), row_of(tiles[1][s], r)) for r in range(SUB)]
        entry = [[lane_of(rows[r], first + c) for c in range(r + 1)] for r in range(SUB)]
        rows = [jnp.where(inside, jnp.where(lane == first + r, 1.0, 0.0), rows[r]) for r in range(SUB)]
        ratio = [[None] * SUB for _ in range(SUB)]
        inverse_pivot = [None] * SUB
        for k in range(SUB):
            inverse_pivot[k] = pl.reciprocal(entry[k][k], approx=True)
            for r in range(k + 1, SUB):
                ratio[r][k] = entry[r][k] * inverse_pivot[k]
            for r in range(k + 1, SUB):
                for c in range(k + 1, r + 1):
                    entry[r][c] = entry[r][c] - ratio[r][k] * entry[c][k]
                rows[r] = rows[r] - ratio[r][k] * rows[k]
        solved = [None] * SUB
        for k in reversed(range(SUB)):
            value = rows[k] * inverse_pivot[k]
            for r in reversed(range(k + 1, SUB)):
                value = value - ratio[r][k] * solved[r]
            solved[k] = value
        for k in range(SUB):
            scaled = jnp.where(lane < first + SUB, rows[k] * lax.rsqrt(entry[k][k]), 0.0)
            for slot in range(2):
                at = slot * (SUB // 2)
                inverse[slot, first + k : first + k + 1, :] = scaled[at : at + 1, :]
        if s + 1 == n_sub:
            break
        for slot in range(2):
            spread = [row_of(solved[k], slot * (SUB // 2)) for k in range(SUB)]
            for i in range(s + 1, n_sub):
                old = tiles[slot][i]
                terms = [lane_of(old, first + c) * spread[c] for c in range(SUB)]
                while len(terms) > 1:
                    terms = [a + b for a, b in zip(terms[::2], terms[1::2])]
                tiles[slot][i] = jnp.where(inside, 0.0, old) - terms[0]


def normal_equations(basis, back, factor, projected, transposed, system):
    order = factor.shape[1]
    width = back.shape[2] // 2
    chunk = 2 * TILE
    for slot in range(2):
        for at in range(0, order, chunk):
            columns = basis[:, slot, :, at : at + chunk].reshape(order, chunk)
            product = jnp.dot(factor[slot], columns, preferred_element_type=F32).astype(BF16)
            projected[slot, :, at : at + chunk] = product
            transposed[slot, at : at + chunk, :] = product.T
        for at in range(0, order, chunk):
            end = at + chunk
            product = jnp.dot(transposed[slot, :end, :], projected[slot, :, at:end], preferred_element_type=F32)
            system[slot, : end // TILE, :, at:end] = product.reshape(end // TILE, TILE, chunk)
        product = jnp.dot(transposed[slot], back[slot], preferred_element_type=F32)
        product = product[:, :width] + product[:, width:]
        system[slot, :, :, order:] = product.reshape(order // TILE, TILE, width)


def finish_block(block, live, inverse, system, out):
    order = out.shape[1]
    first = TILE * (block + 1)
    below = order - first
    for slot in range(2):
        high, low = high_low(inverse[slot])
        left = jnp.concatenate([high, high, low], axis=1)
        high, low = high_low(system[slot, block, :, first:])
        right = jnp.concatenate([high, low, high], axis=0)
        solved = jnp.dot(left, right, preferred_element_type=F32)
        out[slot, first - TILE : first, :] = jnp.where(live[slot] >= 0, solved[:, below:], 0.0)
        if below == 0:
            continue
        high, low = high_low(solved)
        right = jnp.concatenate([high, low, high], axis=0)
        high, low = high_low(solved[:, :below].T)
        left = jnp.concatenate([high, high, low], axis=1)
        end = right.shape[1]
        while end > 0:
            start = max(end - 2 * TILE, 0)
            rows = min(end, below)
            product = jnp.dot(left[:rows], right[:, start:end], preferred_element_type=F32)
            product = product.reshape(rows // TILE, TILE, end - start)
            system[slot, block + 1 : block + 1 + rows // TILE, :, first + start : first + end] -= product
            end = start


def eliminate_kernel(live, place, *refs):
    pieces, basis, back, out = refs[:5], refs[5], refs[6], refs[7]
    factor, projected, transposed, system, work, inverse = refs[8:]
    blocks = out.shape[1] // TILE
    fill_factor(place[0], pieces, factor)
    normal_equations(basis, back, factor, projected, transposed, system)

    def step(j, carry):
        for slot in range(2):
            work[slot] = system[slot, j, :, pl.ds(pl.multiple_of(j * TILE, TILE), TILE)]
        inverse_factors(work, inverse)
        for block in range(blocks):
            pl.when(j == block)(functools.partial(finish_block, block, live, inverse, system, out))
        return carry

    lax.fori_loop(0, blocks, step, 0)


def back_moments(basis, moment):
    order, width = moment.shape[1:]
    return pl.pallas_call(
        back_kernel,
        out_shape=jax.ShapeDtypeStruct((2, order, 2 * width), BF16),
        compiler_params=pltpu.CompilerParams(vmem_limit_bytes=VMEM_BYTES),
        cost_estimate=pl.CostEstimate(flops=8 * order * order * width, bytes_accessed=6 << 20, transcendentals=0),
        name="back_moments",
    )(basis, moment)


def eliminate(live, place, pieces, basis, back):
    _, order, twice = back.shape
    width = twice // 2
    smem = pl.BlockSpec(memory_space=pltpu.SMEM)
    vmem = pl.BlockSpec(memory_space=pltpu.VMEM)
    return pl.pallas_call(
        eliminate_kernel,
        out_shape=jax.ShapeDtypeStruct((2, order, width), F32),
        in_specs=[smem, smem] + [vmem] * 7,
        out_specs=vmem,
        scratch_shapes=[
            pltpu.VMEM((2, order, order), BF16),
            pltpu.VMEM((2, order, order), BF16),
            pltpu.VMEM((2, order, order), BF16),
            pltpu.VMEM((2, order // TILE, TILE, order + width), F32),
            pltpu.VMEM((2, TILE, TILE), F32),
            pltpu.VMEM((2, TILE, TILE), F32),
        ],
        compiler_params=pltpu.CompilerParams(vmem_limit_bytes=VMEM_BYTES),
        cost_estimate=pl.CostEstimate(flops=10 * order**3, bytes_accessed=12 << 20, transcendentals=0),
        name="eliminate",
    )(live, place, *pieces, basis, back)


def on_device(partial_stats, old_basis, exp_avg, slot_block):
    slab_rows, order = partial_stats.shape[2:]
    n_rows = slot_block.shape[0]
    group = lax.axis_index("group")
    own_slots = lax.dynamic_index_in_dim(slot_block, lax.axis_index("dp"), 0, keepdims=False)
    live = (own_slots >= 0)[:, None, None]
    row = lax.broadcasted_iota(jnp.int32, (slab_rows, order), 0) + group * slab_rows
    column = lax.broadcasted_iota(jnp.int32, (slab_rows, order), 1)

    previous = jnp.where(live, old_basis[0], (row == column).astype(BF16)[None])
    basis = lax.all_gather(previous, "group", axis=0)
    back = back_moments(basis, exp_avg[0])

    kept = order // 2 + TILE
    block_start = group * slab_rows // TILE * TILE
    stats = jnp.concatenate([partial_stats[0], partial_stats[0, :, :, : kept - TILE]], axis=2)
    stats = lax.dynamic_slice_in_dim(stats, block_start, kept, axis=2)
    sent = jnp.take(stats, jnp.maximum(slot_block.reshape(-1), 0), axis=0)
    sent = sent.reshape(n_rows, 2, slab_rows, kept)
    shares = lax.all_to_all(sent, "dp", split_axis=0, concat_axis=0)
    identity = (row[:, :kept] == column[:, :kept] + block_start).astype(F32)[None]
    factor = jnp.where(live, jnp.sum(shares.astype(F32), axis=0), identity).astype(BF16)

    place = jnp.stack([group // Z_CHIPS, group % Z_CHIPS]).astype(jnp.int32)
    return eliminate(own_slots, place, gather_factor(factor), basis, back)[None]


def solution(mesh):
    return jax.shard_map(
        on_device,
        mesh=mesh,
        in_specs=(
            P("dp", None, "group", None),
            P("dp", None, "group", None),
            P("dp", None, None, "group"),
            P(),
        ),
        out_specs=P("dp", None, None, "group"),
        check_vma=False,
    )
```

```python
import functools

import jax
import jax.numpy as jnp
from jax import lax
from jax.experimental import pallas as pl
from jax.experimental.pallas import tpu as pltpu
from jax.sharding import PartitionSpec as P

BF16, F32 = jnp.bfloat16, jnp.float32
VMEM_BYTES = 48 * 1024 * 1024
TILE = 128
SUB = 8
X_CHIPS, Z_CHIPS = 4, 8


def high_low(value):
    high = value.astype(BF16)
    return high, (value - high.astype(F32)).astype(BF16)


def from_neighbour(value, dx, dz):
    pairs = []
    for x in range(X_CHIPS):
        for z in range(Z_CHIPS):
            source = (x + dx) % X_CHIPS * Z_CHIPS + (z + dz) % Z_CHIPS
            pairs.append((source, x * Z_CHIPS + z))
    return lax.ppermute(value, "group", pairs)


def gather_factor(slab):
    rows_of_z = [[x * Z_CHIPS + z for z in range(Z_CHIPS)] for x in range(X_CHIPS)]
    copies = jnp.broadcast_to(slab[None], (Z_CHIPS,) + slab.shape)
    own = lax.all_to_all(copies, "group", split_axis=0, concat_axis=0, axis_index_groups=rows_of_z)
    after = from_neighbour(own, 1, 0)
    before = from_neighbour(own, -1, 0)
    half = Z_CHIPS // 2
    across_low = from_neighbour(after[:half], 1, 0)
    across_high = from_neighbour(before[half:], -1, 0)
    return own, after, across_low, across_high, before


def back_kernel(basis, moment, out):
    width = moment.shape[2]
    order = out.shape[1]
    for slot in range(2):
        high, low = high_low(moment[slot])
        both = jnp.concatenate([high, low], axis=1)
        product = jnp.dot(basis[:, slot].reshape(order, order), both, preferred_element_type=F32)
        high, low = high_low(product[:, :width] + product[:, width:])
        out[slot] = jnp.concatenate([high, low], axis=1)


def fill_factor(x, pieces, factor):
    own, after, across_low, across_high, before = pieces
    half = Z_CHIPS // 2
    blocks = factor.shape[1] // TILE
    for distance in range(X_CHIPS):
        for z_half in range(2):
            block_row = lax.rem(x + distance, X_CHIPS) * 2 + z_half
            here = pl.ds(pl.multiple_of(block_row * TILE, TILE), TILE)
            for slot in range(2):
                if distance == 2:
                    piece = (across_low, across_high)[z_half][:, slot]
                else:
                    piece = (own, after, None, before)[distance][half * z_half : half * (z_half + 1), slot]
                piece = piece.reshape(TILE, piece.shape[2])
                for k in range(blocks // 2 + 1):
                    there = pl.ds(pl.multiple_of(lax.rem(block_row + k, blocks) * TILE, TILE), TILE)
                    block = piece[:, TILE * k : TILE * (k + 1)]
                    factor[slot, here, there] = block
                    if 0 < k < blocks // 2:
                        factor[slot, there, here] = block.T


def row_of(value, at):
    return jnp.broadcast_to(value[at : at + 1, :], value.shape)


def lane_of(value, at):
    return jnp.broadcast_to(value[:, at : at + 1], value.shape)


def inverse_factors(work, inverse, errands):
    lane = lax.broadcasted_iota(jnp.int32, (SUB, TILE), 1)
    upper_half = lax.broadcasted_iota(jnp.int32, (SUB, TILE), 0) < SUB // 2
    n_sub = TILE // SUB
    tiles = [[work[slot, SUB * i : SUB * (i + 1), :] for i in range(n_sub)] for slot in range(2)]
    for s in range(n_sub):
        first = SUB * s
        inside = (lane >= first) & (lane < first + SUB)
        rows = [jnp.where(upper_half, row_of(tiles[0][s], r), row_of(tiles[1][s], r)) for r in range(SUB)]
        entry = [[lane_of(rows[r], first + c) for c in range(r + 1)] for r in range(SUB)]
        rows = [jnp.where(inside, jnp.where(lane == first + r, 1.0, 0.0), rows[r]) for r in range(SUB)]
        solved = [None] * SUB
        above = [[None] * SUB for _ in range(SUB)]
        for k in range(SUB):
            pivot_inverse = pl.reciprocal(entry[k][k], approx=True)
            ratio = [entry[r][k] * pivot_inverse if r > k else None for r in range(SUB)]
            for r in range(k + 1, SUB):
                for c in range(k + 1, r + 1):
                    entry[r][c] = entry[r][c] - ratio[r] * entry[c][k]
            scaled = jnp.where(lane < first + SUB, rows[k] * lax.rsqrt(entry[k][k]), 0.0)
            for slot in range(2):
                at = slot * (SUB // 2)
                inverse[slot, first + k : first + k + 1, :] = scaled[at : at + 1, :]
            for r in range(k + 1, SUB):
                rows[r] = rows[r] - ratio[r] * rows[k]
            solved[k] = rows[k] * pivot_inverse
            for r in range(k):
                solved[r] = solved[r] - above[r][k] * solved[k]
                for c in range(k + 1, SUB):
                    above[r][c] = above[r][c] - above[r][k] * ratio[c]
            above[k] = ratio
        if s + 1 < n_sub:
            for slot in range(2):
                spread = [row_of(solved[k], slot * (SUB // 2)) for k in range(SUB)]
                for i in range(s + 1, n_sub):
                    old = tiles[slot][i]
                    terms = [lane_of(old, first + c) * spread[c] for c in range(SUB)]
                    while len(terms) > 1:
                        terms = [a + b for a, b in zip(terms[::2], terms[1::2])]
                    tiles[slot][i] = jnp.where(inside, 0.0, old) - terms[0]
        for errand in errands[s * len(errands) // n_sub : (s + 1) * len(errands) // n_sub]:
            errand()


def project(slot, at, basis, factor, projected, transposed):
    order = factor.shape[1]
    end = at + 2 * TILE
    columns = basis[:, slot, :, at:end].reshape(order, end - at)
    product = jnp.dot(factor[slot], columns, preferred_element_type=F32).astype(BF16)
    projected[slot, :, at:end] = product
    transposed[slot, at:end, :] = product.T


def gram_columns(slot, at, projected, transposed, system):
    end = at + 2 * TILE
    product = jnp.dot(transposed[slot, :end, :], projected[slot, :, at:end], preferred_element_type=F32)
    system[slot, : end // TILE, :, at:end] = product.reshape(end // TILE, TILE, end - at)


def right_side(slot, back, transposed, system):
    order = transposed.shape[1]
    width = back.shape[2] // 2
    product = jnp.dot(transposed[slot], back[slot], preferred_element_type=F32)
    product = product[:, :width] + product[:, width:]
    system[slot, :, :, order:] = product.reshape(order // TILE, TILE, width)


def solve_columns(slot, block, start, end, left, system, panel):
    high, low = high_low(system[slot, block, :, start:end])
    solved = jnp.dot(left[slot], jnp.concatenate([high, low, high], axis=0), preferred_element_type=F32)
    high, low = high_low(solved)
    panel[slot, :TILE, start:end] = high
    panel[slot, TILE : 2 * TILE, start:end] = low
    panel[slot, 2 * TILE :, start:end] = high
    return solved


def take_off(slot, first, last, start, end, panel, across, system):
    left = across[slot, TILE * first : TILE * last, :]
    product = jnp.dot(left, panel[slot, :, start:end], preferred_element_type=F32)
    system[slot, first:last, :, start:end] -= product.reshape(last - first, TILE, end - start)


def turn(slot, block, solved, across):
    high, low = high_low(solved.T)
    across[slot, TILE * block : TILE * (block + 1), :] = jnp.concatenate([high, high, low], axis=1)


def finish_block(block, live, system, out, left, panel, across):
    order = out.shape[1]
    first = TILE * (block + 1)
    errands = []

    def answer(slot):
        solved = solve_columns(slot, block, order, system.shape[3], left, system, panel)
        out[slot, first - TILE : first, :] = jnp.where(live[slot] >= 0, solved, 0.0)

    if first == order:
        for slot in range(2):
            answer(slot)
        return errands
    for slot in range(2):
        solved = solve_columns(slot, block, first, first + TILE, left, system, panel)
        turn(slot, block + 1, solved, across)
    for slot in range(2):
        take_off(slot, block + 1, block + 2, first, first + TILE, panel, across, system)

    def other_columns(slot, start, end):
        solved = solve_columns(slot, block, start, end, left, system, panel)
        for at in range(start, end, TILE):
            turn(slot, at // TILE, solved[:, at - start : at - start + TILE], across)

    chunks = []
    end = order
    while end > first + TILE:
        start = max(end - 2 * TILE, first + TILE)
        chunks.append((start, end))
        end = start
    for slot in range(2):
        errands.append(functools.partial(answer, slot))
        for start, end in chunks:
            errands.append(functools.partial(other_columns, slot, start, end))
    for slot in range(2):
        last = order // TILE
        errands.append(functools.partial(take_off, slot, block + 1, last, order, system.shape[3], panel, across, system))
        for start, end in chunks:
            last = end // TILE
            errands.append(functools.partial(take_off, slot, block + 1, last, start, end, panel, across, system))
    return errands


def eliminate_kernel(live, place, *refs):
    pieces, basis, back, out = refs[:5], refs[5], refs[6], refs[7]
    factor, projected, transposed, system, work, inverse, left, panel, across = refs[8:]
    order = out.shape[1]
    fill_factor(place[0], pieces, factor)
    for slot in range(2):
        for at in range(0, order, 2 * TILE):
            project(slot, at, basis, factor, projected, transposed)
        gram_columns(slot, 0, projected, transposed, system)
    errands = []
    for slot in range(2):
        for at in range(2 * TILE, order, 2 * TILE):
            errands.append(functools.partial(gram_columns, slot, at, projected, transposed, system))
        errands.append(functools.partial(right_side, slot, back, transposed, system))

    for block in range(order // TILE):
        for slot in range(2):
            work[slot] = system[slot, block, :, TILE * block : TILE * (block + 1)]
        inverse_factors(work, inverse, errands)
        for slot in range(2):
            high, low = high_low(inverse[slot])
            left[slot] = jnp.concatenate([high, high, low], axis=1)
        errands = finish_block(block, live, system, out, left, panel, across)


def back_moments(basis, moment):
    order, width = moment.shape[1:]
    return pl.pallas_call(
        back_kernel,
        out_shape=jax.ShapeDtypeStruct((2, order, 2 * width), BF16),
        compiler_params=pltpu.CompilerParams(vmem_limit_bytes=VMEM_BYTES),
        cost_estimate=pl.CostEstimate(flops=8 * order * order * width, bytes_accessed=6 << 20, transcendentals=0),
        name="back_moments",
    )(basis, moment)


def eliminate(live, place, pieces, basis, back):
    _, order, twice = back.shape
    width = twice // 2
    smem = pl.BlockSpec(memory_space=pltpu.SMEM)
    vmem = pl.BlockSpec(memory_space=pltpu.VMEM)
    return pl.pallas_call(
        eliminate_kernel,
        out_shape=jax.ShapeDtypeStruct((2, order, width), F32),
        in_specs=[smem, smem] + [vmem] * 7,
        out_specs=vmem,
        scratch_shapes=[
            pltpu.VMEM((2, order, order), BF16),
            pltpu.VMEM((2, order, order), BF16),
            pltpu.VMEM((2, order, order), BF16),
            pltpu.VMEM((2, order // TILE, TILE, order + width), F32),
            pltpu.VMEM((2, TILE, TILE), F32),
            pltpu.VMEM((2, TILE, TILE), F32),
            pltpu.VMEM((2, TILE, 3 * TILE), BF16),
            pltpu.VMEM((2, 3 * TILE, order + width), BF16),
            pltpu.VMEM((2, order, 3 * TILE), BF16),
        ],
        compiler_params=pltpu.CompilerParams(vmem_limit_bytes=VMEM_BYTES),
        cost_estimate=pl.CostEstimate(flops=10 * order**3, bytes_accessed=12 << 20, transcendentals=0),
        name="eliminate",
    )(live, place, *pieces, basis, back)


def on_device(partial_stats, old_basis, exp_avg, slot_block):
    slab_rows, order = partial_stats.shape[2:]
    n_rows = slot_block.shape[0]
    group = lax.axis_index("group")

    basis = lax.all_gather(old_basis[0], "group", axis=0)
    back = back_moments(basis, exp_avg[0])

    kept = order // 2 + TILE
    block_start = group * slab_rows // TILE * TILE
    stats = jnp.concatenate([partial_stats[0], partial_stats[0, :, :, : kept - TILE]], axis=2)
    stats = lax.dynamic_slice_in_dim(stats, block_start, kept, axis=2)
    sent = jnp.take(stats, jnp.maximum(slot_block.reshape(-1), 0), axis=0, mode="clip")
    sent = sent.reshape(n_rows, 2, slab_rows, kept)
    shares = lax.all_to_all(sent, "dp", split_axis=0, concat_axis=0)
    factor = jnp.sum(shares.astype(F32), axis=0).astype(BF16)

    own_slots = lax.dynamic_index_in_dim(slot_block, lax.axis_index("dp"), 0, keepdims=False)
    place = jnp.stack([group // Z_CHIPS, group % Z_CHIPS]).astype(jnp.int32)
    return eliminate(own_slots, place, gather_factor(factor), basis, back)[None]


def solution(mesh):
    return jax.shard_map(
        on_device,
        mesh=mesh,
        in_specs=(
            P("dp", None, "group", None),
            P("dp", None, "group", None),
            P("dp", None, None, "group"),
            P(),
        ),
        out_specs=P("dp", None, None, "group"),
        check_vma=False,
    )
```

```python
import functools

import jax
import jax.numpy as jnp
from jax import lax
from jax.experimental import pallas as pl
from jax.experimental.pallas import tpu as pltpu
from jax.sharding import PartitionSpec as P

BF16, F32 = jnp.bfloat16, jnp.float32
VMEM_BYTES = 48 * 1024 * 1024
TILE = 128
SUB = 8
X_CHIPS, Z_CHIPS = 4, 8


def high_low(value):
    high = value.astype(BF16)
    return high, (value - high.astype(F32)).astype(BF16)


def from_neighbour(value, dx, dz):
    pairs = []
    for x in range(X_CHIPS):
        for z in range(Z_CHIPS):
            source = (x + dx) % X_CHIPS * Z_CHIPS + (z + dz) % Z_CHIPS
            pairs.append((source, x * Z_CHIPS + z))
    return lax.ppermute(value, "group", pairs)


def gather_factor(slab):
    rows_of_z = [[x * Z_CHIPS + z for z in range(Z_CHIPS)] for x in range(X_CHIPS)]
    copies = jnp.broadcast_to(slab[None], (Z_CHIPS,) + slab.shape)
    own = lax.all_to_all(copies, "group", split_axis=0, concat_axis=0, axis_index_groups=rows_of_z)
    after = from_neighbour(own, 1, 0)
    before = from_neighbour(own, -1, 0)
    half = Z_CHIPS // 2
    across_low = from_neighbour(after[:half], 1, 0)
    across_high = from_neighbour(before[half:], -1, 0)
    return own, after, across_low, across_high, before


def back_kernel(basis, moment, out):
    width = moment.shape[2]
    order = out.shape[1]
    for slot in range(2):
        high, low = high_low(moment[slot])
        both = jnp.concatenate([high, low], axis=1)
        product = jnp.dot(basis[:, slot].reshape(order, order), both, preferred_element_type=F32)
        high, low = high_low(product[:, :width] + product[:, width:])
        out[slot] = jnp.concatenate([high, low], axis=1)


def fill_factor(x, pieces, factor):
    own, after, across_low, across_high, before = pieces
    half = Z_CHIPS // 2
    blocks = factor.shape[1] // TILE
    for distance in range(X_CHIPS):
        for z_half in range(2):
            block_row = lax.rem(x + distance, X_CHIPS) * 2 + z_half
            here = pl.ds(pl.multiple_of(block_row * TILE, TILE), TILE)
            for slot in range(2):
                if distance == 2:
                    piece = (across_low, across_high)[z_half][:, slot]
                else:
                    piece = (own, after, None, before)[distance][half * z_half : half * (z_half + 1), slot]
                piece = piece.reshape(TILE, piece.shape[2])
                for k in range(blocks // 2 + 1):
                    there = pl.ds(pl.multiple_of(lax.rem(block_row + k, blocks) * TILE, TILE), TILE)
                    block = piece[:, TILE * k : TILE * (k + 1)]
                    factor[slot, here, there] = block
                    if 0 < k < blocks // 2:
                        factor[slot, there, here] = block.T


def row_of(value, at):
    return jnp.broadcast_to(value[at : at + 1, :], value.shape)


def lane_of(value, at):
    return jnp.broadcast_to(value[:, at : at + 1], value.shape)


def inverse_factors(work, inverse):
    lane = lax.broadcasted_iota(jnp.int32, (SUB, TILE), 1)
    upper_half = lax.broadcasted_iota(jnp.int32, (SUB, TILE), 0) < SUB // 2
    n_sub = TILE // SUB
    tiles, scales = [], []
    diagonal = lax.broadcasted_iota(jnp.int32, (TILE, TILE), 0) == lax.broadcasted_iota(jnp.int32, (TILE, TILE), 1)
    for slot in range(2):
        matrix = work[slot]
        pivots = jnp.where(diagonal, matrix, 0.0)
        scale = lax.rsqrt(jnp.sum(pivots, axis=0, keepdims=True))
        matrix = matrix * lax.rsqrt(jnp.sum(pivots, axis=1, keepdims=True)) * scale
        tiles.append([matrix[SUB * i : SUB * (i + 1), :] for i in range(n_sub)])
        scales.append(jnp.broadcast_to(scale, (SUB, TILE)))
    scale = jnp.where(upper_half, scales[0], scales[1])
    for s in range(n_sub):
        first = SUB * s
        inside = (lane >= first) & (lane < first + SUB)
        done = jnp.where(lane < first + SUB, scale, 0.0)
        rows = [jnp.where(upper_half, row_of(tiles[0][s], r), row_of(tiles[1][s], r)) for r in range(SUB)]
        entry = [[lane_of(rows[r], first + c) for c in range(r + 1)] for r in range(SUB)]
        rows = [jnp.where(inside, jnp.where(lane == first + r, 1.0, 0.0), rows[r]) for r in range(SUB)]
        solved = [None] * SUB
        above = [None] * SUB
        for p in range(0, SUB, 2):
            q = p + 1
            a, b, c = entry[p][p], entry[q][p], entry[q][q]
            r = pl.reciprocal(a * c - b * b, approx=True)
            ratio_p, ratio_q = [None] * SUB, [None] * SUB
            for t in range(q + 1, SUB):
                ratio_p[t] = (entry[t][p] * c - entry[t][q] * b) * r
                ratio_q[t] = (entry[t][q] * a - entry[t][p] * b) * r
            for t in range(q + 1, SUB):
                for u in range(q + 1, t + 1):
                    entry[t][u] = entry[t][u] - (ratio_p[t] * entry[u][p] + ratio_q[t] * entry[u][q])
            root = lax.rsqrt(a)
            lower = b * (root * root)
            second = rows[q] - lower * rows[p]
            finished = (rows[p] * root * done, second * lax.rsqrt(c - b * lower) * done)
            for slot in range(2):
                at = slot * (SUB // 2)
                for k in range(2):
                    inverse[slot, first + p + k : first + p + k + 1, :] = finished[k][at : at + 1, :]
            solved[p] = rows[p] * (c * r) - rows[q] * (b * r)
            solved[q] = rows[q] * (a * r) - rows[p] * (b * r)
            for t in range(q + 1, SUB):
                rows[t] = rows[t] - (ratio_p[t] * rows[p] + ratio_q[t] * rows[q])
            for t in range(p):
                solved[t] = solved[t] - (above[t][p] * solved[p] + above[t][q] * solved[q])
                for u in range(q + 1, SUB):
                    above[t][u] = above[t][u] - (above[t][p] * ratio_p[u] + above[t][q] * ratio_q[u])
            above[p], above[q] = ratio_p, ratio_q
        if s + 1 == n_sub:
            break
        for slot in range(2):
            spread = [row_of(solved[k], slot * (SUB // 2)) for k in range(SUB)]
            for i in range(s + 1, n_sub):
                old = tiles[slot][i]
                terms = [lane_of(old, first + c) * spread[c] for c in range(SUB)]
                while len(terms) > 1:
                    terms = [a + b for a, b in zip(terms[::2], terms[1::2])]
                tiles[slot][i] = jnp.where(inside, 0.0, old) - terms[0]


def normal_equations(basis, back, factor, projected, transposed, system):
    order = factor.shape[1]
    width = back.shape[2] // 2
    chunk = 2 * TILE
    for slot in range(2):
        for at in range(0, order, chunk):
            columns = basis[:, slot, :, at : at + chunk].reshape(order, chunk)
            product = jnp.dot(factor[slot], columns, preferred_element_type=F32).astype(BF16)
            projected[slot, :, at : at + chunk] = product
            transposed[slot, at : at + chunk, :] = product.T
        for at in range(0, order, chunk):
            end = at + chunk
            product = jnp.dot(transposed[slot, :end, :], projected[slot, :, at:end], preferred_element_type=F32)
            system[slot, : end // TILE, :, at:end] = product.reshape(end // TILE, TILE, chunk)
        product = jnp.dot(transposed[slot], back[slot], preferred_element_type=F32)
        product = product[:, :width] + product[:, width:]
        system[slot, :, :, order:] = product.reshape(order // TILE, TILE, width)


def finish_block(block, live, inverse, system, out):
    order = out.shape[1]
    first = TILE * (block + 1)
    below = order - first
    for slot in range(2):
        high, low = high_low(inverse[slot])
        left = jnp.concatenate([high, high, low], axis=1)
        high, low = high_low(system[slot, block, :, first:])
        right = jnp.concatenate([high, low, high], axis=0)
        solved = jnp.dot(left, right, preferred_element_type=F32)
        out[slot, first - TILE : first, :] = jnp.where(live[slot] >= 0, solved[:, below:], 0.0)
        if below == 0:
            continue
        high, low = high_low(solved)
        right = jnp.concatenate([high, low, high], axis=0)
        high, low = high_low(solved[:, :below].T)
        left = jnp.concatenate([high, high, low], axis=1)
        end = right.shape[1]
        while end > 0:
            start = max(end - 2 * TILE, 0)
            rows = min(end, below)
            product = jnp.dot(left[:rows], right[:, start:end], preferred_element_type=F32)
            product = product.reshape(rows // TILE, TILE, end - start)
            system[slot, block + 1 : block + 1 + rows // TILE, :, first + start : first + end] -= product
            end = start


def eliminate_kernel(live, place, *refs):
    pieces, basis, back, out = refs[:5], refs[5], refs[6], refs[7]
    factor, projected, transposed, system, work, inverse = refs[8:]
    blocks = out.shape[1] // TILE
    fill_factor(place[0], pieces, factor)
    normal_equations(basis, back, factor, projected, transposed, system)

    def step(j, carry):
        for slot in range(2):
            work[slot] = system[slot, j, :, pl.ds(pl.multiple_of(j * TILE, TILE), TILE)]
        inverse_factors(work, inverse)
        for block in range(blocks):
            pl.when(j == block)(functools.partial(finish_block, block, live, inverse, system, out))
        return carry

    lax.fori_loop(0, blocks, step, 0)


def back_moments(basis, moment):
    order, width = moment.shape[1:]
    return pl.pallas_call(
        back_kernel,
        out_shape=jax.ShapeDtypeStruct((2, order, 2 * width), BF16),
        compiler_params=pltpu.CompilerParams(vmem_limit_bytes=VMEM_BYTES),
        cost_estimate=pl.CostEstimate(flops=8 * order * order * width, bytes_accessed=6 << 20, transcendentals=0),
        name="back_moments",
    )(basis, moment)


def eliminate(live, place, pieces, basis, back):
    _, order, twice = back.shape
    width = twice // 2
    smem = pl.BlockSpec(memory_space=pltpu.SMEM)
    vmem = pl.BlockSpec(memory_space=pltpu.VMEM)
    return pl.pallas_call(
        eliminate_kernel,
        out_shape=jax.ShapeDtypeStruct((2, order, width), F32),
        in_specs=[smem, smem] + [vmem] * 7,
        out_specs=vmem,
        scratch_shapes=[
            pltpu.VMEM((2, order, order), BF16),
            pltpu.VMEM((2, order, order), BF16),
            pltpu.VMEM((2, order, order), BF16),
            pltpu.VMEM((2, order // TILE, TILE, order + width), F32),
            pltpu.VMEM((2, TILE, TILE), F32),
            pltpu.VMEM((2, TILE, TILE), F32),
        ],
        compiler_params=pltpu.CompilerParams(vmem_limit_bytes=VMEM_BYTES),
        cost_estimate=pl.CostEstimate(flops=10 * order**3, bytes_accessed=12 << 20, transcendentals=0),
        name="eliminate",
    )(live, place, *pieces, basis, back)


def on_device(partial_stats, old_basis, exp_avg, slot_block):
    slab_rows, order = partial_stats.shape[2:]
    n_rows = slot_block.shape[0]
    group = lax.axis_index("group")

    basis = lax.all_gather(old_basis[0], "group", axis=0)
    back = back_moments(basis, exp_avg[0])

    kept = order // 2 + TILE
    block_start = group * slab_rows // TILE * TILE
    stats = jnp.concatenate([partial_stats[0], partial_stats[0, :, :, : kept - TILE]], axis=2)
    stats = lax.dynamic_slice_in_dim(stats, block_start, kept, axis=2)

    core = lax.rem(lax.axis_index("dp"), 2)
    blocks = jnp.maximum(slot_block, 0).reshape(n_rows // 2, 2, 2)

    def shares_for(core):
        wanted = lax.dynamic_index_in_dim(blocks, core, 1, keepdims=False).reshape(-1)
        return jnp.take(stats, wanted, axis=0, mode="clip").reshape(n_rows // 2, 2, slab_rows, kept)

    other = lax.ppermute(shares_for(1 - core), "dp", [(d, d ^ 1) for d in range(n_rows)])
    pairs = (shares_for(core).astype(F32) + other.astype(F32)).astype(BF16)
    same_core = [list(range(c, n_rows, 2)) for c in range(2)]
    shares = lax.all_to_all(pairs, "dp", split_axis=0, concat_axis=0, axis_index_groups=same_core)
    factor = jnp.sum(shares.astype(F32), axis=0).astype(BF16)

    own_slots = lax.dynamic_index_in_dim(slot_block, lax.axis_index("dp"), 0, keepdims=False)
    place = jnp.stack([group // Z_CHIPS, group % Z_CHIPS]).astype(jnp.int32)
    return eliminate(own_slots, place, gather_factor(factor), basis, back)[None]


def solution(mesh):
    return jax.shard_map(
        on_device,
        mesh=mesh,
        in_specs=(
            P("dp", None, "group", None),
            P("dp", None, "group", None),
            P("dp", None, None, "group"),
            P(),
        ),
        out_specs=P("dp", None, None, "group"),
        check_vma=False,
    )
```

```python
import functools

import jax
import jax.numpy as jnp
from jax import lax
from jax.experimental import pallas as pl
from jax.experimental.pallas import tpu as pltpu
from jax.sharding import PartitionSpec as P

BF16, F32 = jnp.bfloat16, jnp.float32
VMEM_BYTES = 48 * 1024 * 1024
TILE = 128
SUB = 8
PANEL = 32
X_CHIPS, Z_CHIPS = 4, 8
ALONG_Z = [[x * Z_CHIPS + z for z in range(Z_CHIPS)] for x in range(X_CHIPS)]
ALONG_X = [[x * Z_CHIPS + z for x in range(X_CHIPS)] for z in range(Z_CHIPS)]


def high_low(value):
    high = value.astype(BF16)
    return high, (value - high.astype(F32)).astype(BF16)


def from_neighbour(value, dx, dz):
    pairs = []
    for x in range(X_CHIPS):
        for z in range(Z_CHIPS):
            source = (x + dx) % X_CHIPS * Z_CHIPS + (z + dz) % Z_CHIPS
            pairs.append((source, x * Z_CHIPS + z))
    return lax.ppermute(value, "group", pairs)


def gather_factor(slab):
    copies = jnp.broadcast_to(slab[None], (Z_CHIPS,) + slab.shape)
    own = lax.all_to_all(copies, "group", split_axis=0, concat_axis=0, axis_index_groups=ALONG_Z)
    after = from_neighbour(own, 1, 0)
    before = from_neighbour(own, -1, 0)
    half = Z_CHIPS // 2
    across_low = from_neighbour(after[:half], 1, 0)
    across_high = from_neighbour(before[half:], -1, 0)
    return own, after, across_low, across_high, before


def fill_factor(x, pieces, factor):
    own, after, across_low, across_high, before = pieces
    half = Z_CHIPS // 2
    blocks = factor.shape[1] // TILE
    for distance in range(X_CHIPS):
        for z_half in range(2):
            block_row = lax.rem(x + distance, X_CHIPS) * 2 + z_half
            here = pl.ds(pl.multiple_of(block_row * TILE, TILE), TILE)
            for slot in range(2):
                if distance == 2:
                    piece = (across_low, across_high)[z_half][:, slot]
                else:
                    piece = (own, after, None, before)[distance][half * z_half : half * (z_half + 1), slot]
                piece = piece.reshape(TILE, piece.shape[2])
                for k in range(blocks // 2 + 1):
                    there = pl.ds(pl.multiple_of(lax.rem(block_row + k, blocks) * TILE, TILE), TILE)
                    block = piece[:, TILE * k : TILE * (k + 1)]
                    factor[slot, here, there] = block
                    if 0 < k < blocks // 2:
                        factor[slot, there, here] = block.T


def row_of(value, at):
    return jnp.broadcast_to(value[at : at + 1, :], value.shape)


def lane_of(value, at):
    return jnp.broadcast_to(value[:, at : at + 1], value.shape)


def inverse_factors(work, done, inverse):
    lane = lax.broadcasted_iota(jnp.int32, (SUB, TILE), 1)
    upper_half = lax.broadcasted_iota(jnp.int32, (SUB, TILE), 0) < SUB // 2
    whole_row = lax.broadcasted_iota(jnp.int32, (TILE, TILE), 0)
    whole_lane = lax.broadcasted_iota(jnp.int32, (TILE, TILE), 1)
    scales = []
    for slot in range(2):
        matrix = work[slot]
        pivots = jnp.where(whole_row == whole_lane, matrix, 0.0)
        scale = lax.rsqrt(jnp.sum(pivots, axis=0, keepdims=True))
        work[slot] = matrix * lax.rsqrt(jnp.sum(pivots, axis=1, keepdims=True)) * scale
        scales.append(scale)
    for panel in range(0, TILE, PANEL):
        n_sub = PANEL // SUB
        tiles = [[work[slot, panel + SUB * i : panel + SUB * (i + 1), :] for i in range(n_sub)] for slot in range(2)]
        for s in range(n_sub):
            eliminate_rows(tiles, s, panel + SUB * s, lane, upper_half, done)
        end = panel + PANEL
        if end == TILE:
            break
        row = whole_row[:PANEL] + panel
        inner = whole_lane[:PANEL] < end
        below = whole_lane[: TILE - end]
        for slot in range(2):
            rows = done[slot, panel:end, :]
            rows = jnp.where(inner & (whole_lane[:PANEL] > row), 0.0, rows)
            high, low = high_low(rows)
            left = jnp.concatenate([high, high, low], axis=0).astype(F32).T[end:, :].astype(BF16)
            product = jnp.dot(left, jnp.concatenate([high, low, high], axis=0), preferred_element_type=F32)
            old = jnp.where((below >= panel) & (below < end), 0.0, work[slot, end:, :])
            work[slot, end:, :] = old - product
    for slot in range(2):
        inverse[slot] = jnp.where(whole_lane <= whole_row, done[slot] * scales[slot], 0.0)


def eliminate_rows(tiles, s, first, lane, upper_half, done):
    inside = (lane >= first) & (lane < first + SUB)
    rows = [jnp.where(upper_half, row_of(tiles[0][s], r), row_of(tiles[1][s], r)) for r in range(SUB)]
    entry = [[lane_of(rows[r], first + c) for c in range(r + 1)] for r in range(SUB)]
    rows = [jnp.where(inside, jnp.where(lane == first + r, 1.0, 0.0), rows[r]) for r in range(SUB)]
    more = s + 1 < len(tiles[0])
    solved = [None] * SUB
    above = [None] * SUB
    for p in range(0, SUB, 2):
        q = p + 1
        a, b, c = entry[p][p], entry[q][p], entry[q][q]
        r = pl.reciprocal(a * c - b * b, approx=True)
        ratio_p, ratio_q = [None] * SUB, [None] * SUB
        for t in range(q + 1, SUB):
            ratio_p[t] = (entry[t][p] * c - entry[t][q] * b) * r
            ratio_q[t] = (entry[t][q] * a - entry[t][p] * b) * r
        for t in range(q + 1, SUB):
            for u in range(q + 1, t + 1):
                entry[t][u] = entry[t][u] - (ratio_p[t] * entry[u][p] + ratio_q[t] * entry[u][q])
        root = lax.rsqrt(a)
        lower = b * (root * root)
        finished = (rows[p] * root, (rows[q] - lower * rows[p]) * lax.rsqrt(c - b * lower))
        for slot in range(2):
            at = slot * (SUB // 2)
            for k in range(2):
                done[slot, first + p + k : first + p + k + 1, :] = finished[k][at : at + 1, :]
        for t in range(q + 1, SUB):
            rows[t] = rows[t] - (ratio_p[t] * rows[p] + ratio_q[t] * rows[q])
        if not more:
            continue
        solved[p] = rows[p] * (c * r) - rows[q] * (b * r)
        solved[q] = rows[q] * (a * r) - rows[p] * (b * r)
        for t in range(p):
            solved[t] = solved[t] - (above[t][p] * solved[p] + above[t][q] * solved[q])
            for u in range(q + 1, SUB):
                above[t][u] = above[t][u] - (above[t][p] * ratio_p[u] + above[t][q] * ratio_q[u])
        above[p], above[q] = ratio_p, ratio_q
    if not more:
        return
    for slot in range(2):
        spread = [row_of(solved[k], slot * (SUB // 2)) for k in range(SUB)]
        for i in range(s + 1, len(tiles[slot])):
            old = tiles[slot][i]
            terms = [lane_of(old, first + c) * spread[c] for c in range(SUB)]
            while len(terms) > 1:
                terms = [a + b for a, b in zip(terms[::2], terms[1::2])]
            tiles[slot][i] = jnp.where(inside, 0.0, old) - terms[0]


def normal_equations(basis, moment, factor, projected, transposed, system):
    order = factor.shape[1]
    width = moment.shape[2]
    chunk = 2 * TILE
    for slot in range(2):
        for at in range(0, order, chunk):
            columns = basis[:, slot, :, at : at + chunk].reshape(order, chunk)
            product = jnp.dot(factor[slot], columns, preferred_element_type=F32).astype(BF16)
            projected[slot, :, at : at + chunk] = product
            transposed[slot, at : at + chunk, :] = product.T
        for at in range(0, order, chunk):
            end = at + chunk
            product = jnp.dot(transposed[slot, :end, :], projected[slot, :, at:end], preferred_element_type=F32)
            system[slot, : end // TILE, :, at:end] = product.reshape(end // TILE, TILE, chunk)
        product = moment[slot]
        for left in (basis[:, slot].reshape(order, order), transposed[slot]):
            product = jnp.dot(left, jnp.concatenate(high_low(product), axis=1), preferred_element_type=F32)
            product = product[:, :width] + product[:, width:]
        system[slot, :, :, order:] = product.reshape(order // TILE, TILE, width)


def finish_block(block, live, inverse, system, out):
    order = out.shape[1]
    first = TILE * (block + 1)
    below = order - first
    for slot in range(2):
        high, low = high_low(inverse[slot])
        left = jnp.concatenate([high, high, low], axis=1)
        high, low = high_low(system[slot, block, :, first:])
        right = jnp.concatenate([high, low, high], axis=0)
        solved = jnp.dot(left, right, preferred_element_type=F32)
        out[slot, first - TILE : first, :] = jnp.where(live[slot] >= 0, solved[:, below:], 0.0)
        if below == 0:
            continue
        high, low = high_low(solved)
        right = jnp.concatenate([high, low, high], axis=0)
        high, low = high_low(solved[:, :below].T)
        left = jnp.concatenate([high, high, low], axis=1)
        end = right.shape[1]
        while end > 0:
            start = max(end - 2 * TILE, 0)
            rows = min(end, below)
            product = jnp.dot(left[:rows], right[:, start:end], preferred_element_type=F32)
            product = product.reshape(rows // TILE, TILE, end - start)
            system[slot, block + 1 : block + 1 + rows // TILE, :, first + start : first + end] -= product
            end = start


def eliminate_kernel(live, place, *refs):
    pieces, basis, moment, out = refs[:5], refs[5], refs[6], refs[7]
    factor, projected, transposed, system, work, done, inverse = refs[8:]
    blocks = out.shape[1] // TILE
    fill_factor(place[0], pieces, factor)
    normal_equations(basis, moment, factor, projected, transposed, system)

    def step(j, carry):
        for slot in range(2):
            work[slot] = system[slot, j, :, pl.ds(pl.multiple_of(j * TILE, TILE), TILE)]
        inverse_factors(work, done, inverse)
        for block in range(blocks):
            pl.when(j == block)(functools.partial(finish_block, block, live, inverse, system, out))
        return carry

    lax.fori_loop(0, blocks, step, 0)


def eliminate(live, place, pieces, basis, moment):
    _, order, width = moment.shape
    smem = pl.BlockSpec(memory_space=pltpu.SMEM)
    vmem = pl.BlockSpec(memory_space=pltpu.VMEM)
    return pl.pallas_call(
        eliminate_kernel,
        out_shape=jax.ShapeDtypeStruct((2, order, width), F32),
        in_specs=[smem, smem] + [vmem] * 7,
        out_specs=vmem,
        scratch_shapes=[
            pltpu.VMEM((2, order, order), BF16),
            pltpu.VMEM((2, order, order), BF16),
            pltpu.VMEM((2, order, order), BF16),
            pltpu.VMEM((2, order // TILE, TILE, order + width), F32),
            pltpu.VMEM((2, TILE, TILE), F32),
            pltpu.VMEM((2, TILE, TILE), F32),
            pltpu.VMEM((2, TILE, TILE), F32),
        ],
        compiler_params=pltpu.CompilerParams(vmem_limit_bytes=VMEM_BYTES),
        cost_estimate=pl.CostEstimate(flops=10 * order**3, bytes_accessed=12 << 20, transcendentals=0),
        name="eliminate",
    )(live, place, *pieces, basis, moment)


def on_device(partial_stats, old_basis, exp_avg, slot_block):
    slab_rows, order = partial_stats.shape[2:]
    n_rows = slot_block.shape[0]
    group = lax.axis_index("group")

    basis = lax.all_gather(old_basis[0], "group", axis=0, axis_index_groups=ALONG_Z)

    kept = order // 2 + TILE
    block_start = group * slab_rows // TILE * TILE
    stats = jnp.concatenate([partial_stats[0], partial_stats[0, :, :, : kept - TILE]], axis=2)
    stats = lax.dynamic_slice_in_dim(stats, block_start, kept, axis=2)

    core = lax.rem(lax.axis_index("dp"), 2)
    blocks = jnp.maximum(slot_block, 0).reshape(n_rows // 2, 2, 2)

    def shares_for(core):
        wanted = lax.dynamic_index_in_dim(blocks, core, 1, keepdims=False).reshape(-1)
        return jnp.take(stats, wanted, axis=0, mode="clip").reshape(n_rows // 2, 2, slab_rows, kept)

    other = lax.ppermute(shares_for(1 - core), "dp", [(d, d ^ 1) for d in range(n_rows)])
    pairs = (shares_for(core).astype(F32) + other.astype(F32)).astype(BF16)
    same_core = [list(range(c, n_rows, 2)) for c in range(2)]
    shares = lax.all_to_all(pairs, "dp", split_axis=0, concat_axis=0, axis_index_groups=same_core)
    shares, basis = lax.optimization_barrier((shares, basis))
    basis = lax.all_gather(basis, "group", axis=0, axis_index_groups=ALONG_X)
    basis = basis.reshape((X_CHIPS * Z_CHIPS,) + basis.shape[2:])
    factor = jnp.sum(shares.astype(F32), axis=0).astype(BF16)

    own_slots = lax.dynamic_index_in_dim(slot_block, lax.axis_index("dp"), 0, keepdims=False)
    place = jnp.stack([group // Z_CHIPS, group % Z_CHIPS]).astype(jnp.int32)
    return eliminate(own_slots, place, gather_factor(factor), basis, exp_avg[0])[None]


def solution(mesh):
    return jax.shard_map(
        on_device,
        mesh=mesh,
        in_specs=(
            P("dp", None, "group", None),
            P("dp", None, "group", None),
            P("dp", None, None, "group"),
            P(),
        ),
        out_specs=P("dp", None, None, "group"),
        check_vma=False,
    )
```

```python
import functools

import jax
import jax.numpy as jnp
from jax import lax
from jax.experimental import pallas as pl
from jax.experimental.pallas import tpu as pltpu
from jax.sharding import PartitionSpec as P

BF16, F32 = jnp.bfloat16, jnp.float32
VMEM_BYTES = 48 * 1024 * 1024
TILE = 128
SUB = 8
PANEL = 32
X_CHIPS, Z_CHIPS = 4, 8
ALONG_Z = [[x * Z_CHIPS + z for z in range(Z_CHIPS)] for x in range(X_CHIPS)]


def high_low(value):
    high = value.astype(BF16)
    return high, (value - high.astype(F32)).astype(BF16)


def from_neighbour(value, dx, dz):
    pairs = []
    for x in range(X_CHIPS):
        for z in range(Z_CHIPS):
            source = (x + dx) % X_CHIPS * Z_CHIPS + (z + dz) % Z_CHIPS
            pairs.append((source, x * Z_CHIPS + z))
    return lax.ppermute(value, "group", pairs)


def gather_factor(slab):
    copies = jnp.broadcast_to(slab[None], (Z_CHIPS,) + slab.shape)
    own = lax.all_to_all(copies, "group", split_axis=0, concat_axis=0, axis_index_groups=ALONG_Z)
    after = from_neighbour(own, 1, 0)
    before = from_neighbour(own, -1, 0)
    half = Z_CHIPS // 2
    across_low = from_neighbour(after[:half], 1, 0)
    across_high = from_neighbour(before[half:], -1, 0)
    return own, after, across_low, across_high, before


def fill_kernel(place, *refs):
    x, pieces, factor = place[0], refs[:5], refs[5]
    own, after, across_low, across_high, before = pieces
    half = Z_CHIPS // 2
    blocks = factor.shape[1] // TILE
    for distance in range(X_CHIPS):
        for z_half in range(2):
            block_row = lax.rem(x + distance, X_CHIPS) * 2 + z_half
            here = pl.ds(pl.multiple_of(block_row * TILE, TILE), TILE)
            for slot in range(2):
                if distance == 2:
                    piece = (across_low, across_high)[z_half][:, slot]
                else:
                    piece = (own, after, None, before)[distance][half * z_half : half * (z_half + 1), slot]
                piece = piece.reshape(TILE, piece.shape[2])
                for k in range(blocks // 2 + 1):
                    there = pl.ds(pl.multiple_of(lax.rem(block_row + k, blocks) * TILE, TILE), TILE)
                    block = piece[:, TILE * k : TILE * (k + 1)]
                    factor[slot, here, there] = block
                    if 0 < k < blocks // 2:
                        factor[slot, there, here] = block.T


def row_of(value, at):
    return jnp.broadcast_to(value[at : at + 1, :], value.shape)


def lane_of(value, at):
    return jnp.broadcast_to(value[:, at : at + 1], value.shape)


def inverse_factors(work, done, inverse):
    lane = lax.broadcasted_iota(jnp.int32, (SUB, TILE), 1)
    upper_half = lax.broadcasted_iota(jnp.int32, (SUB, TILE), 0) < SUB // 2
    whole_row = lax.broadcasted_iota(jnp.int32, (TILE, TILE), 0)
    whole_lane = lax.broadcasted_iota(jnp.int32, (TILE, TILE), 1)
    scales = []
    for slot in range(2):
        matrix = work[slot]
        pivots = jnp.where(whole_row == whole_lane, matrix, 0.0)
        scale = lax.rsqrt(jnp.sum(pivots, axis=0, keepdims=True))
        work[slot] = matrix * lax.rsqrt(jnp.sum(pivots, axis=1, keepdims=True)) * scale
        scales.append(scale)
    for panel in range(0, TILE, PANEL):
        n_sub = PANEL // SUB
        tiles = [[work[slot, panel + SUB * i : panel + SUB * (i + 1), :] for i in range(n_sub)] for slot in range(2)]
        for s in range(n_sub):
            eliminate_rows(tiles, s, panel + SUB * s, lane, upper_half, done)
        end = panel + PANEL
        if end == TILE:
            break
        row = whole_row[:PANEL] + panel
        inner = whole_lane[:PANEL] < end
        below = whole_lane[: TILE - end]
        for slot in range(2):
            rows = done[slot, panel:end, :]
            rows = jnp.where(inner & (whole_lane[:PANEL] > row), 0.0, rows)
            high, low = high_low(rows)
            left = jnp.concatenate([high, high, low], axis=0).astype(F32).T[end:, :].astype(BF16)
            product = jnp.dot(left, jnp.concatenate([high, low, high], axis=0), preferred_element_type=F32)
            old = jnp.where((below >= panel) & (below < end), 0.0, work[slot, end:, :])
            work[slot, end:, :] = old - product
    for slot in range(2):
        inverse[slot] = jnp.where(whole_lane <= whole_row, done[slot] * scales[slot], 0.0)


def eliminate_rows(tiles, s, first, lane, upper_half, done):
    inside = (lane >= first) & (lane < first + SUB)
    rows = [jnp.where(upper_half, row_of(tiles[0][s], r), row_of(tiles[1][s], r)) for r in range(SUB)]
    entry = [[lane_of(rows[r], first + c) for c in range(r + 1)] for r in range(SUB)]
    rows = [jnp.where(inside, jnp.where(lane == first + r, 1.0, 0.0), rows[r]) for r in range(SUB)]
    more = s + 1 < len(tiles[0])
    solved = [None] * SUB
    above = [None] * SUB
    for p in range(0, SUB, 2):
        q = p + 1
        a, b, c = entry[p][p], entry[q][p], entry[q][q]
        r = pl.reciprocal(a * c - b * b, approx=True)
        ratio_p, ratio_q = [None] * SUB, [None] * SUB
        for t in range(q + 1, SUB):
            ratio_p[t] = (entry[t][p] * c - entry[t][q] * b) * r
            ratio_q[t] = (entry[t][q] * a - entry[t][p] * b) * r
        for t in range(q + 1, SUB):
            for u in range(q + 1, t + 1):
                entry[t][u] = entry[t][u] - (ratio_p[t] * entry[u][p] + ratio_q[t] * entry[u][q])
        root = lax.rsqrt(a)
        lower = b * (root * root)
        finished = (rows[p] * root, (rows[q] - lower * rows[p]) * lax.rsqrt(c - b * lower))
        for slot in range(2):
            at = slot * (SUB // 2)
            for k in range(2):
                done[slot, first + p + k : first + p + k + 1, :] = finished[k][at : at + 1, :]
        for t in range(q + 1, SUB):
            rows[t] = rows[t] - (ratio_p[t] * rows[p] + ratio_q[t] * rows[q])
        if not more:
            continue
        solved[p] = rows[p] * (c * r) - rows[q] * (b * r)
        solved[q] = rows[q] * (a * r) - rows[p] * (b * r)
        for t in range(p):
            solved[t] = solved[t] - (above[t][p] * solved[p] + above[t][q] * solved[q])
            for u in range(q + 1, SUB):
                above[t][u] = above[t][u] - (above[t][p] * ratio_p[u] + above[t][q] * ratio_q[u])
        above[p], above[q] = ratio_p, ratio_q
    if not more:
        return
    for slot in range(2):
        spread = [row_of(solved[k], slot * (SUB // 2)) for k in range(SUB)]
        for i in range(s + 1, len(tiles[slot])):
            old = tiles[slot][i]
            terms = [lane_of(old, first + c) * spread[c] for c in range(SUB)]
            while len(terms) > 1:
                terms = [a + b for a, b in zip(terms[::2], terms[1::2])]
            tiles[slot][i] = jnp.where(inside, 0.0, old) - terms[0]


def normal_equations(basis, moment, factor, projected, transposed, system):
    order = factor.shape[1]
    width = moment.shape[2]
    chunk = 2 * TILE
    for slot in range(2):
        for at in range(0, order, chunk):
            columns = basis[:, slot, :, at : at + chunk].reshape(order, chunk)
            product = jnp.dot(factor[slot], columns, preferred_element_type=F32).astype(BF16)
            projected[slot, :, at : at + chunk] = product
            transposed[slot, at : at + chunk, :] = product.T
        for at in range(0, order, chunk):
            end = at + chunk
            product = jnp.dot(transposed[slot, :end, :], projected[slot, :, at:end], preferred_element_type=F32)
            system[slot, : end // TILE, :, at:end] = product.reshape(end // TILE, TILE, chunk)
        product = moment[slot]
        for left in (basis[:, slot].reshape(order, order), transposed[slot]):
            product = jnp.dot(left, jnp.concatenate(high_low(product), axis=1), preferred_element_type=F32)
            product = product[:, :width] + product[:, width:]
        system[slot, :, :, order:] = product.reshape(order // TILE, TILE, width)


def finish_block(block, live, inverse, system, out):
    order = out.shape[1]
    first = TILE * (block + 1)
    below = order - first
    for slot in range(2):
        high, low = high_low(inverse[slot])
        left = jnp.concatenate([high, high, low], axis=1)
        high, low = high_low(system[slot, block, :, first:])
        right = jnp.concatenate([high, low, high], axis=0)
        solved = jnp.dot(left, right, preferred_element_type=F32)
        out[slot, first - TILE : first, :] = jnp.where(live[slot] >= 0, solved[:, below:], 0.0)
        if below == 0:
            continue
        high, low = high_low(solved)
        right = jnp.concatenate([high, low, high], axis=0)
        high, low = high_low(solved[:, :below].T)
        left = jnp.concatenate([high, high, low], axis=1)
        end = right.shape[1]
        while end > 0:
            start = max(end - 2 * TILE, 0)
            rows = min(end, below)
            product = jnp.dot(left[:rows], right[:, start:end], preferred_element_type=F32)
            product = product.reshape(rows // TILE, TILE, end - start)
            system[slot, block + 1 : block + 1 + rows // TILE, :, first + start : first + end] -= product
            end = start


def eliminate_kernel(live, factor, basis, moment, out, *scratch):
    projected, transposed, system, work, done, inverse = scratch
    blocks = out.shape[1] // TILE
    normal_equations(basis, moment, factor, projected, transposed, system)

    def step(j, carry):
        for slot in range(2):
            work[slot] = system[slot, j, :, pl.ds(pl.multiple_of(j * TILE, TILE), TILE)]
        inverse_factors(work, done, inverse)
        for block in range(blocks):
            pl.when(j == block)(functools.partial(finish_block, block, live, inverse, system, out))
        return carry

    lax.fori_loop(0, blocks, step, 0)


def whole_factor(place, pieces):
    order = X_CHIPS * Z_CHIPS * pieces[0].shape[2]
    smem = pl.BlockSpec(memory_space=pltpu.SMEM)
    vmem = pl.BlockSpec(memory_space=pltpu.VMEM)
    return pl.pallas_call(
        fill_kernel,
        out_shape=jax.ShapeDtypeStruct((2, order, order), BF16),
        in_specs=[smem] + [vmem] * 5,
        out_specs=vmem,
        compiler_params=pltpu.CompilerParams(vmem_limit_bytes=VMEM_BYTES),
        cost_estimate=pl.CostEstimate(flops=0, bytes_accessed=7 << 20, transcendentals=0),
        name="whole_factor",
    )(place, *pieces)


def eliminate(live, factor, basis, moment):
    _, order, width = moment.shape
    smem = pl.BlockSpec(memory_space=pltpu.SMEM)
    vmem = pl.BlockSpec(memory_space=pltpu.VMEM)
    return pl.pallas_call(
        eliminate_kernel,
        out_shape=jax.ShapeDtypeStruct((2, order, width), F32),
        in_specs=[smem] + [vmem] * 3,
        out_specs=vmem,
        scratch_shapes=[
            pltpu.VMEM((2, order, order), BF16),
            pltpu.VMEM((2, order, order), BF16),
            pltpu.VMEM((2, order // TILE, TILE, order + width), F32),
            pltpu.VMEM((2, TILE, TILE), F32),
            pltpu.VMEM((2, TILE, TILE), F32),
            pltpu.VMEM((2, TILE, TILE), F32),
        ],
        compiler_params=pltpu.CompilerParams(vmem_limit_bytes=VMEM_BYTES),
        cost_estimate=pl.CostEstimate(flops=10 * order**3, bytes_accessed=12 << 20, transcendentals=0),
        name="eliminate",
    )(live, factor, basis, moment)


def on_device(partial_stats, old_basis, exp_avg, slot_block):
    slab_rows, order = partial_stats.shape[2:]
    n_rows = slot_block.shape[0]
    group = lax.axis_index("group")

    basis = lax.all_gather(old_basis[0], "group", axis=0)

    kept = order // 2 + TILE
    block_start = group * slab_rows // TILE * TILE
    stats = jnp.concatenate([partial_stats[0], partial_stats[0, :, :, : kept - TILE]], axis=2)
    stats = lax.dynamic_slice_in_dim(stats, block_start, kept, axis=2)

    core = lax.rem(lax.axis_index("dp"), 2)
    blocks = jnp.maximum(slot_block, 0).reshape(n_rows // 2, 2, 2)

    def shares_for(core):
        wanted = lax.dynamic_index_in_dim(blocks, core, 1, keepdims=False).reshape(-1)
        return jnp.take(stats, wanted, axis=0, mode="clip").reshape(n_rows // 2, 2, slab_rows, kept)

    other = lax.ppermute(shares_for(1 - core), "dp", [(d, d ^ 1) for d in range(n_rows)])
    pairs = (shares_for(core).astype(F32) + other.astype(F32)).astype(BF16)
    same_core = [list(range(c, n_rows, 2)) for c in range(2)]
    shares = lax.all_to_all(pairs, "dp", split_axis=0, concat_axis=0, axis_index_groups=same_core)
    factor = jnp.sum(shares.astype(F32), axis=0).astype(BF16)

    own_slots = lax.dynamic_index_in_dim(slot_block, lax.axis_index("dp"), 0, keepdims=False)
    place = jnp.stack([group // Z_CHIPS, group % Z_CHIPS]).astype(jnp.int32)
    factor = whole_factor(place, gather_factor(factor))
    return eliminate(own_slots, factor, basis, exp_avg[0])[None]


def solution(mesh):
    return jax.shard_map(
        on_device,
        mesh=mesh,
        in_specs=(
            P("dp", None, "group", None),
            P("dp", None, "group", None),
            P("dp", None, None, "group"),
            P(),
        ),
        out_specs=P("dp", None, None, "group"),
        check_vma=False,
    )
```

```python
import functools

import jax
import jax.numpy as jnp
from jax import lax
from jax.experimental import pallas as pl
from jax.experimental.pallas import tpu as pltpu
from jax.sharding import PartitionSpec as P

BF16, F32 = jnp.bfloat16, jnp.float32
VMEM_BYTES = 48 * 1024 * 1024
TILE = 128
SUB = 8
PANEL = 32
X_CHIPS, Z_CHIPS = 4, 8
ALONG_Z = [[x * Z_CHIPS + z for z in range(Z_CHIPS)] for x in range(X_CHIPS)]


def high_low(value):
    high = value.astype(BF16)
    return high, (value - high.astype(F32)).astype(BF16)


def from_neighbour(value, dx, dz):
    pairs = []
    for x in range(X_CHIPS):
        for z in range(Z_CHIPS):
            source = (x + dx) % X_CHIPS * Z_CHIPS + (z + dz) % Z_CHIPS
            pairs.append((source, x * Z_CHIPS + z))
    return lax.ppermute(value, "group", pairs)


def gather_factor(slab):
    copies = jnp.broadcast_to(slab[None], (Z_CHIPS,) + slab.shape)
    own = lax.all_to_all(copies, "group", split_axis=0, concat_axis=0, axis_index_groups=ALONG_Z)
    low, high = own[: Z_CHIPS // 2], own[Z_CHIPS // 2 :]
    after_low = from_neighbour(low, 1, 0)
    before_high = from_neighbour(high, -1, 0)
    after_high = from_neighbour(high, 1, 0)
    before_low = from_neighbour(low, -1, 0)
    across_low = from_neighbour(after_low, 1, 0)
    across_high = from_neighbour(before_high, -1, 0)
    return own, after_low, after_high, across_low, across_high, before_low, before_high


def fill_factor(x, pieces, factor):
    half = Z_CHIPS // 2
    blocks = factor.shape[1] // TILE
    for distance in range(X_CHIPS):
        for z_half in range(2):
            block_row = lax.rem(x + distance, X_CHIPS) * 2 + z_half
            here = pl.ds(pl.multiple_of(block_row * TILE, TILE), TILE)
            for slot in range(2):
                if distance == 0:
                    piece = pieces[0][half * z_half : half * (z_half + 1), slot]
                else:
                    piece = pieces[2 * distance - 1 + z_half][:, slot]
                piece = piece.reshape(TILE, piece.shape[2])
                for k in range(blocks // 2 + 1):
                    there = pl.ds(pl.multiple_of(lax.rem(block_row + k, blocks) * TILE, TILE), TILE)
                    block = piece[:, TILE * k : TILE * (k + 1)]
                    factor[slot, here, there] = block
                    if 0 < k < blocks // 2:
                        factor[slot, there, here] = block.T


def row_of(value, at):
    return jnp.broadcast_to(value[at : at + 1, :], value.shape)


def lane_of(value, at):
    return jnp.broadcast_to(value[:, at : at + 1], value.shape)


def inverse_factors(work, done, inverse):
    lane = lax.broadcasted_iota(jnp.int32, (SUB, TILE), 1)
    upper_half = lax.broadcasted_iota(jnp.int32, (SUB, TILE), 0) < SUB // 2
    whole_row = lax.broadcasted_iota(jnp.int32, (TILE, TILE), 0)
    whole_lane = lax.broadcasted_iota(jnp.int32, (TILE, TILE), 1)
    scales = []
    for slot in range(2):
        matrix = work[slot]
        pivots = jnp.where(whole_row == whole_lane, matrix, 0.0)
        scale = lax.rsqrt(jnp.sum(pivots, axis=0, keepdims=True))
        work[slot] = matrix * lax.rsqrt(jnp.sum(pivots, axis=1, keepdims=True)) * scale
        scales.append(scale)
    for panel in range(0, TILE, PANEL):
        n_sub = PANEL // SUB
        tiles = [[work[slot, panel + SUB * i : panel + SUB * (i + 1), :] for i in range(n_sub)] for slot in range(2)]
        for s in range(n_sub):
            eliminate_rows(tiles, s, panel + SUB * s, lane, upper_half, done)
        end = panel + PANEL
        if end == TILE:
            break
        row = whole_row[:PANEL] + panel
        inner = whole_lane[:PANEL] < end
        below = whole_lane[: TILE - end]
        for slot in range(2):
            rows = done[slot, panel:end, :]
            rows = jnp.where(inner & (whole_lane[:PANEL] > row), 0.0, rows)
            high, low = high_low(rows)
            left = jnp.concatenate([high, high, low], axis=0).astype(F32).T[end:, :].astype(BF16)
            product = jnp.dot(left, jnp.concatenate([high, low, high], axis=0), preferred_element_type=F32)
            old = jnp.where((below >= panel) & (below < end), 0.0, work[slot, end:, :])
            work[slot, end:, :] = old - product
    for slot in range(2):
        inverse[slot] = jnp.where(whole_lane <= whole_row, done[slot] * scales[slot], 0.0)


def eliminate_rows(tiles, s, first, lane, upper_half, done):
    inside = (lane >= first) & (lane < first + SUB)
    rows = [jnp.where(upper_half, row_of(tiles[0][s], r), row_of(tiles[1][s], r)) for r in range(SUB)]
    entry = [[lane_of(rows[r], first + c) for c in range(r + 1)] for r in range(SUB)]
    rows = [jnp.where(inside, jnp.where(lane == first + r, 1.0, 0.0), rows[r]) for r in range(SUB)]
    more = s + 1 < len(tiles[0])
    solved = [None] * SUB
    above = [None] * SUB
    for p in range(0, SUB, 2):
        q = p + 1
        a, b, c = entry[p][p], entry[q][p], entry[q][q]
        r = pl.reciprocal(a * c - b * b, approx=True)
        ratio_p, ratio_q = [None] * SUB, [None] * SUB
        for t in range(q + 1, SUB):
            ratio_p[t] = (entry[t][p] * c - entry[t][q] * b) * r
            ratio_q[t] = (entry[t][q] * a - entry[t][p] * b) * r
        for t in range(q + 1, SUB):
            for u in range(q + 1, t + 1):
                entry[t][u] = entry[t][u] - (ratio_p[t] * entry[u][p] + ratio_q[t] * entry[u][q])
        root = lax.rsqrt(a)
        lower = b * (root * root)
        finished = (rows[p] * root, (rows[q] - lower * rows[p]) * lax.rsqrt(c - b * lower))
        for slot in range(2):
            at = slot * (SUB // 2)
            for k in range(2):
                done[slot, first + p + k : first + p + k + 1, :] = finished[k][at : at + 1, :]
        for t in range(q + 1, SUB):
            rows[t] = rows[t] - (ratio_p[t] * rows[p] + ratio_q[t] * rows[q])
        if not more:
            continue
        solved[p] = rows[p] * (c * r) - rows[q] * (b * r)
        solved[q] = rows[q] * (a * r) - rows[p] * (b * r)
        for t in range(p):
            solved[t] = solved[t] - (above[t][p] * solved[p] + above[t][q] * solved[q])
            for u in range(q + 1, SUB):
                above[t][u] = above[t][u] - (above[t][p] * ratio_p[u] + above[t][q] * ratio_q[u])
        above[p], above[q] = ratio_p, ratio_q
    if not more:
        return
    for slot in range(2):
        spread = [row_of(solved[k], slot * (SUB // 2)) for k in range(SUB)]
        for i in range(s + 1, len(tiles[slot])):
            old = tiles[slot][i]
            terms = [lane_of(old, first + c) * spread[c] for c in range(SUB)]
            while len(terms) > 1:
                terms = [a + b for a, b in zip(terms[::2], terms[1::2])]
            tiles[slot][i] = jnp.where(inside, 0.0, old) - terms[0]


def normal_equations(basis, moment, factor, projected, transposed, system):
    order = factor.shape[1]
    width = moment.shape[2]
    chunk = 2 * TILE
    for slot in range(2):
        for at in range(0, order, chunk):
            columns = basis[:, slot, :, at : at + chunk].reshape(order, chunk)
            product = jnp.dot(factor[slot], columns, preferred_element_type=F32).astype(BF16)
            projected[slot, :, at : at + chunk] = product
            transposed[slot, at : at + chunk, :] = product.T
        for at in range(0, order, chunk):
            end = at + chunk
            product = jnp.dot(transposed[slot, :end, :], projected[slot, :, at:end], preferred_element_type=F32)
            system[slot, : end // TILE, :, at:end] = product.reshape(end // TILE, TILE, chunk)
        product = moment[slot]
        for left in (basis[:, slot].reshape(order, order), transposed[slot]):
            product = jnp.dot(left, jnp.concatenate(high_low(product), axis=1), preferred_element_type=F32)
            product = product[:, :width] + product[:, width:]
        system[slot, :, :, order:] = product.reshape(order // TILE, TILE, width)


def finish_block(block, live, inverse, system, out):
    order = out.shape[1]
    first = TILE * (block + 1)
    below = order - first
    for slot in range(2):
        high, low = high_low(inverse[slot])
        left = jnp.concatenate([high, high, low], axis=1)
        high, low = high_low(system[slot, block, :, first:])
        right = jnp.concatenate([high, low, high], axis=0)
        solved = jnp.dot(left, right, preferred_element_type=F32)
        out[slot, first - TILE : first, :] = jnp.where(live[slot] >= 0, solved[:, below:], 0.0)
        if below == 0:
            continue
        high, low = high_low(solved)
        right = jnp.concatenate([high, low, high], axis=0)
        high, low = high_low(solved[:, :below].T)
        left = jnp.concatenate([high, high, low], axis=1)
        end = right.shape[1]
        while end > 0:
            start = max(end - 2 * TILE, 0)
            rows = min(end, below)
            product = jnp.dot(left[:rows], right[:, start:end], preferred_element_type=F32)
            product = product.reshape(rows // TILE, TILE, end - start)
            system[slot, block + 1 : block + 1 + rows // TILE, :, first + start : first + end] -= product
            end = start


def eliminate_kernel(live, place, *refs):
    pieces, basis, moment, out = refs[:7], refs[7], refs[8], refs[9]
    factor, projected, transposed, system, work, done, inverse = refs[10:]
    blocks = out.shape[1] // TILE
    fill_factor(place[0], pieces, factor)
    normal_equations(basis, moment, factor, projected, transposed, system)

    def step(j, carry):
        for slot in range(2):
            work[slot] = system[slot, j, :, pl.ds(pl.multiple_of(j * TILE, TILE), TILE)]
        inverse_factors(work, done, inverse)
        for block in range(blocks):
            pl.when(j == block)(functools.partial(finish_block, block, live, inverse, system, out))
        return carry

    lax.fori_loop(0, blocks, step, 0)


def eliminate(live, place, pieces, basis, moment):
    _, order, width = moment.shape
    smem = pl.BlockSpec(memory_space=pltpu.SMEM)
    vmem = pl.BlockSpec(memory_space=pltpu.VMEM)
    return pl.pallas_call(
        eliminate_kernel,
        out_shape=jax.ShapeDtypeStruct((2, order, width), F32),
        in_specs=[smem, smem] + [vmem] * 9,
        out_specs=vmem,
        scratch_shapes=[
            pltpu.VMEM((2, order, order), BF16),
            pltpu.VMEM((2, order, order), BF16),
            pltpu.VMEM((2, order, order), BF16),
            pltpu.VMEM((2, order // TILE, TILE, order + width), F32),
            pltpu.VMEM((2, TILE, TILE), F32),
            pltpu.VMEM((2, TILE, TILE), F32),
            pltpu.VMEM((2, TILE, TILE), F32),
        ],
        compiler_params=pltpu.CompilerParams(vmem_limit_bytes=VMEM_BYTES),
        cost_estimate=pl.CostEstimate(flops=10 * order**3, bytes_accessed=12 << 20, transcendentals=0),
        name="eliminate",
    )(live, place, *pieces, basis, moment)


def on_device(partial_stats, old_basis, exp_avg, slot_block):
    slab_rows, order = partial_stats.shape[2:]
    n_rows = slot_block.shape[0]
    group = lax.axis_index("group")

    basis = lax.all_gather(old_basis[0], "group", axis=0)

    kept = order // 2 + TILE
    block_start = group * slab_rows // TILE * TILE
    stats = jnp.concatenate([partial_stats[0], partial_stats[0, :, :, : kept - TILE]], axis=2)
    stats = lax.dynamic_slice_in_dim(stats, block_start, kept, axis=2)

    core = lax.rem(lax.axis_index("dp"), 2)
    blocks = jnp.maximum(slot_block, 0).reshape(n_rows // 2, 2, 2)

    def shares_for(core):
        wanted = lax.dynamic_index_in_dim(blocks, core, 1, keepdims=False).reshape(-1)
        return jnp.take(stats, wanted, axis=0, mode="clip").reshape(n_rows // 2, 2, slab_rows, kept)

    other = lax.ppermute(shares_for(1 - core), "dp", [(d, d ^ 1) for d in range(n_rows)])
    pairs = (shares_for(core).astype(F32) + other.astype(F32)).astype(BF16)
    same_core = [list(range(c, n_rows, 2)) for c in range(2)]
    shares = lax.all_to_all(pairs, "dp", split_axis=0, concat_axis=0, axis_index_groups=same_core)
    factor = jnp.sum(shares.astype(F32), axis=0).astype(BF16)

    own_slots = lax.dynamic_index_in_dim(slot_block, lax.axis_index("dp"), 0, keepdims=False)
    place = jnp.stack([group // Z_CHIPS, group % Z_CHIPS]).astype(jnp.int32)
    return eliminate(own_slots, place, gather_factor(factor), basis, exp_avg[0])[None]


def solution(mesh):
    return jax.shard_map(
        on_device,
        mesh=mesh,
        in_specs=(
            P("dp", None, "group", None),
            P("dp", None, "group", None),
            P("dp", None, None, "group"),
            P(),
        ),
        out_specs=P("dp", None, None, "group"),
        check_vma=False,
    )
```
